32 devices in a mesh: grp: 1, ep: 16 (over z, y, x), sub: 2 (over core).
Axes of the slice: x: 2, y: 2, z: 4, core: 2. Of those that a mesh axis runs over, the one named last changes fastest.
Arguments:
- resid_in: bfloat16 [2048, 2048], P(('grp', 'ep', 'sub')), may hold values from -6 to 6
- query_input: bfloat16 [2048, 1024], P(('grp', 'ep', 'sub')), may hold values from -6 to 6
- key_input: bfloat16 [2048, 1024], P(('grp', 'ep', 'sub')), may hold values from -6 to 6
- value_input: bfloat16 [2048, 2048], P(('grp', 'ep', 'sub')), may hold values from -6 to 6
- gate_input: bfloat16 [2048, 2048], P(('grp', 'ep', 'sub')), may hold values from -6 to 6
- decay_log: float32 [16, 2048], P(None, ('grp', 'ep', 'sub')), may hold values from -1 to 0
- write_rate: float32 [16, 2048], P(None, ('grp', 'ep', 'sub')), may hold values from 0.05 to 0.95
- segments: int32 [32, 64], P(('grp', 'ep', 'sub')), may hold values from 0 to 3, never falling along the last dimension, each value on 1 to 32 neighbouring positions
- head_gain: float32 [128], replicated, may hold values from 0.1 to 1.9
- out_proj: bfloat16 [2048, 2048], P('sub'), may hold values from -0.125 to 0.125
- post_gain: float32 [2048], replicated, may hold values from 0.1 to 1.9
- block_exps: int32 [2048, 16], P(('grp', 'ep', 'sub')), may hold values from -9 to -5
- route_ids: int32 [2048, 10], P(('grp', 'ep', 'sub')), may hold values from 0 to 31, all different within a row; in each aligned block of 64 rows (0 to 63, 64 to 127, ...) at most 32 rows name the same one
- route_weights: float32 [2048, 10], P(('grp', 'ep', 'sub')), may hold values from 0.1 to 1
- w_gate_up: bfloat16 [32, 2048, 1024], P(('ep', 'sub')), may hold values from -0.125 to 0.125
- w_down: bfloat16 [32, 512, 2048], P(('ep', 'sub')), may hold values from -0.25 to 0.25
Outputs:
- layer_out: bfloat16 [2048, 2048], P(('grp', 'ep', 'sub'))
The draws below stay inside these ranges and needn't reach their ends.
Inputs may be any that keep to these rules, and one draw needn't show every extreme that they name: `route_ids`: on the rows of one device no expert is named more than 32 times, a bound that some block reaches. `segments`: each device's row numbers its own sequences from 0 and never falls; a sequence has at most 32 tokens, and some has exactly that many.
All inputs are finite; a program needn't handle non-finite values.
Results may differ from the reference program's by a relative error of at most 0.014.
Values may be sent and summed in bfloat16 or wider, within the bound.
A program may use at most 128 MiB of HBM per device.

```python
import math
import jax
import jax.numpy as jnp
import numpy as np
from jax import lax

D = 2048
KH = 8
HALF_VALUE_HEADS = 16
DK = 128
DV = 128
FFE = 512
TOPK = 10
QBLOCK = 128
TOK_DEV = 64
TOKENS_PER_BATCH = 2048
EXPERTS = 32
CAP = 32
N_EP = 16
N_SUB = 2


def draw_decay_log(key, part):
    key = jax.random.fold_in(key, 7)
    random_child_keys = jax.random.split(key, 5)
    lowest, highest = (math.log(1.0 / 400.0), math.log(1.0 / 8.0))
    resting_rate = jnp.exp(jax.random.uniform(random_child_keys[0], (HALF_VALUE_HEADS, 1), jnp.float32, lowest, highest))
    processor_factor = jnp.exp(jax.random.uniform(random_child_keys[1], (HALF_VALUE_HEADS, TOKENS_PER_BATCH // TOK_DEV), jnp.float32, math.log(0.5), math.log(2.0)))
    processor_factor = jnp.repeat(processor_factor, TOK_DEV, axis=1)
    roughness = jax.random.uniform(random_child_keys[2], (HALF_VALUE_HEADS, TOKENS_PER_BATCH), jnp.float32, 0.5, 1.5)
    spike_mask = jax.random.bernoulli(random_child_keys[3], 0.08, (HALF_VALUE_HEADS, TOKENS_PER_BATCH))
    spike_penalty = jnp.log(jax.random.uniform(random_child_keys[4], (HALF_VALUE_HEADS, TOKENS_PER_BATCH), jnp.float32, 0.3, 0.7))
    grand_total = -resting_rate * processor_factor * roughness + jnp.where(spike_mask, spike_penalty, 0.0)
    return jnp.maximum(grand_total, -1.0)


def plant(result, key, smallest, top_value):
    place = [jax.random.randint(jax.random.fold_in(key, axis), (), 0, length) for axis, length in enumerate(result.shape)]
    main_axis = result.shape.index(max(result.shape))
    neighbour = place[:main_axis] + [(place[main_axis] + 1) % result.shape[main_axis]] + place[main_axis + 1:]
    return result.at[tuple(place)].set(smallest).at[tuple(neighbour)].set(top_value)


def shard_levels(rng, shape, cuts, least, high):
    def one(axis_at, parts):
        steps = jax.random.uniform(jax.random.fold_in(jax.random.fold_in(rng, 6), axis_at), (parts,), jnp.float32, least / len(cuts), high / len(cuts))
        return jnp.repeat(jnp.exp(steps), shape[axis_at] // parts).reshape((-1,) + (1,) * (len(shape) - axis_at - 1))

    loudness = one(*cuts[0])
    for cut in cuts[1:]:
        loudness = loudness * one(*cut)
    return loudness


def split_up(count, total, bound, skew):
    loads = [(1 << 20) // math.isqrt(rank ** skew) + 1 for rank in range(2, count + 1)]
    surplus, given = total - bound - (count - 1), [1] * (count - 1)
    while surplus > 0:
        movable = [i for i in range(count - 1) if given[i] < bound]
        mass, left = sum([loads[i] for i in movable]), surplus
        for i in movable:
            more = min(bound - given[i], max(1, left * loads[i] // mass), surplus)
            given[i] = given[i] + more
            surplus = surplus - more
    return np.array([bound] + given)


def ragged_sizes(own_key, number_of, total, most, lean):
    if number_of == 2:
        one = jax.random.randint(own_key, (), max(1, total - most), min(most, total - 1) + 1)
        return jnp.stack([one, total - one])
    lengths = jnp.asarray(split_up(number_of, total, most, lean), jnp.int32)
    pairs = (number_of - 1) // 2
    source_of, receiver = lengths[1:1 + 2 * pairs:2], lengths[2:2 + 2 * pairs:2]
    margin = jnp.minimum(source_of - 1, most - receiver)
    moved = jax.random.randint(jax.random.fold_in(own_key, 1), (pairs,), 0, 1 << 20) % (margin + 1)
    lengths = lengths.at[1:1 + 2 * pairs:2].set(source_of - moved).at[2:2 + 2 * pairs:2].set(receiver + moved)
    return lengths[jax.random.permutation(jax.random.fold_in(own_key, 2), number_of)]


def shared_out(own_key, own, number, rows, number_of, top, reach, slope):
    sequence = jax.random.permutation(own_key, number_of)
    crowded, ordinary = load_shares(number_of, rows * top, reach, slope, True), load_shares(number_of, rows * top, reach, slope, False)
    places = jnp.arange(number_of)

    def named(tallies, rotation):
        used = int((tallies > 0).sum())
        fixed = max(1, used // 4)
        passed = fixed + (places - fixed + rotation * (used - fixed)) % max(1, number_of - fixed)
        return jnp.zeros((number_of,), jnp.int32).at[sequence[jnp.where(places < fixed, places, passed)]].set(jnp.asarray(tallies, jnp.int32))

    tallies = jnp.where(number % 4 == 0, named(crowded, number // 4), named(ordinary, number - number // 4 - 1))
    mixed = jax.random.permutation(jax.random.fold_in(own, 3), number_of)
    giver, receiver = mixed[0:number_of // 2 * 2:2], mixed[1:number_of // 2 * 2:2]
    room = jnp.minimum(tallies[giver] - 1, reach - tallies[receiver]) // 2
    room = jnp.where((giver == sequence[0]) | (receiver == sequence[0]) | (tallies[receiver] == 0), 0, jnp.maximum(room, 0))
    passed = jax.random.randint(jax.random.fold_in(own, 4), (number_of // 2,), 0, 1 << 20) % (room + 1)
    tallies = tallies.at[giver].add(-passed).at[receiver].add(passed)
    labels = jnp.searchsorted(jnp.cumsum(tallies), jnp.arange(rows * top), side="right").astype(jnp.int32)
    listing = labels.reshape(top, rows).T
    listing = listing[jax.random.permutation(jax.random.fold_in(own, 1), rows)]
    rotation = jax.random.randint(jax.random.fold_in(own, 2), (rows, 1), 0, top)
    return jnp.take_along_axis(listing, (jnp.arange(top)[None, :] + rotation) % top, axis=1)


def load_shares(amount, total, limit, slope, full):
    portions = [(1 << 20) // math.isqrt(standing ** slope) + 1 for standing in range(1, amount + 1)]
    largest = limit if full else min(limit, max(-(-total // amount), total * portions[0] // sum(portions)))
    least = 1 if total - largest >= amount - 1 else 0
    counts, spare = [largest] + [least] * (amount - 1), total - largest - least * (amount - 1)
    while spare > 0:
        candidates = [i for i in range(1, amount) if counts[i] < largest] or [i for i in range(1, amount) if counts[i] < limit]
        mass, left = sum([portions[i] for i in candidates]), spare
        for i in candidates:
            extra = min(limit - counts[i], max(1, left * portions[i] // mass), spare)
            counts[i] = counts[i] + extra
            spare = spare - extra
    return np.array(counts)


def normal_values(own_key, extent, scale, limit, pieces=(), kind=jnp.bfloat16):
    values = jax.random.normal(own_key, extent, jnp.float32) * scale
    if len(pieces) > 0:
        values = shard_levels(own_key, extent, pieces, -0.22, 0.18) * values
    return jnp.clip(values, min=-limit, max=limit).astype(kind)


def setup_inputs(seed: int = 0, part: int = 0) -> dict:
    splits = jax.random.split(jax.random.key(seed), 17)
    part_splits = jax.random.split(jax.random.fold_in(splits[16], part), 17)
    resid_in = normal_values(part_splits[0], (TOKENS_PER_BATCH, D), 1.0, 6.0, ((0, 32),))
    query_input = normal_values(part_splits[1], (TOKENS_PER_BATCH, KH * DK), 1.0, 6.0, ((0, 32),))
    key_input = normal_values(part_splits[2], (TOKENS_PER_BATCH, KH * DK), 1.0, 6.0, ((0, 32),))
    value_input = normal_values(part_splits[3], (TOKENS_PER_BATCH, HALF_VALUE_HEADS * DV), 1.0, 6.0, ((0, 32),))
    gate_input = normal_values(part_splits[4], (TOKENS_PER_BATCH, HALF_VALUE_HEADS * DV), 1.0, 6.0, ((0, 32),))
    decay_log = draw_decay_log(jax.random.fold_in(jax.random.fold_in(splits[16], part), 71), part)
    write_rate = jnp.clip(0.05 + 0.9 * jax.random.uniform(part_splits[6], (HALF_VALUE_HEADS, TOKENS_PER_BATCH), jnp.float32) ** shard_levels(part_splits[6], (HALF_VALUE_HEADS, TOKENS_PER_BATCH), ((1, 32),), -0.2, 0.2), 0.05, 0.95)
    segments = jax.vmap(lambda own: jnp.searchsorted(jnp.cumsum(ragged_sizes(own, max(3, TOK_DEV // 16), TOK_DEV, TOK_DEV // 2, 2)), jnp.arange(TOK_DEV), side="right"))(jax.random.split(part_splits[7], (N_EP * N_SUB))).reshape((N_EP * N_SUB, TOK_DEV)).astype(jnp.int32)
    head_gain = jnp.clip(1.0 + 0.18 * jax.random.normal(splits[8], (DV,), jnp.float32), 0.1, 1.9)
    out_proj = normal_values(splits[9], (HALF_VALUE_HEADS * DV, D), (HALF_VALUE_HEADS * DV) ** -0.5, 0.125, ((0, 2),))
    post_gain = jnp.clip(1.0 + 0.18 * jax.random.normal(splits[10], (D,), jnp.float32), 0.1, 1.9)
    block_exps = plant(jax.random.randint(part_splits[11], (TOKENS_PER_BATCH, D // QBLOCK), -9, -4), jax.random.fold_in(part_splits[11], 1), -9, (-4) - 1).astype(jnp.int32)
    route_ids_keys = jax.random.split(jax.random.fold_in(part_splits[12], 1), TOKENS_PER_BATCH // TOK_DEV)
    route_ids_turns = jax.random.permutation(jax.random.fold_in(part_splits[12], 3), TOKENS_PER_BATCH // TOK_DEV)
    route_ids = jax.vmap(lambda own, number: shared_out(jax.random.fold_in(part_splits[12], 2), own, number, TOK_DEV, EXPERTS, TOPK, CAP, 2))(route_ids_keys, route_ids_turns).reshape((TOKENS_PER_BATCH, TOPK))
    route_weights = jnp.clip(jnp.exp(math.log(1.0) - 2.3025851 * jax.random.uniform(part_splits[13], (TOKENS_PER_BATCH, TOPK), jnp.float32) ** shard_levels(part_splits[13], (TOKENS_PER_BATCH, TOPK), ((0, 32),), -0.2, 0.2)), 0.1, 1.0)
    w_gate_up = normal_values(splits[14], (EXPERTS, D, 2 * FFE), D ** -0.5, 0.125, ((0, 32),))
    w_down = normal_values(splits[15], (EXPERTS, FFE, D), FFE ** -0.5, 0.25, ((0, 32),))
    return dict(resid_in=resid_in, query_input=query_input, key_input=key_input, value_input=value_input, gate_input=gate_input, decay_log=decay_log, write_rate=write_rate, segments=segments, head_gain=head_gain, out_proj=out_proj, post_gain=post_gain, block_exps=block_exps, route_ids=route_ids, route_weights=route_weights, w_gate_up=w_gate_up, w_down=w_down)


def unit_rows(values_in):
    return values_in * lax.rsqrt(lax.optimization_barrier(jnp.sum(values_in * values_in, -1, keepdims=True)) + 1e-06)

def reference(resid_in, query_input, key_input, value_input, gate_input, decay_log, write_rate, segments, head_gain, out_proj, post_gain, block_exps, route_ids, route_weights, w_gate_up, w_down):
    devices = N_EP * N_SUB
    tokens = resid_in.shape[0]
    repeat = HALF_VALUE_HEADS // KH
    query_heads = jnp.repeat(unit_rows(query_input.astype(jnp.float32).reshape(tokens, KH, DK)), repeat, axis=1)
    key_heads = jnp.repeat(unit_rows(key_input.astype(jnp.float32).reshape(tokens, KH, DK)), repeat, axis=1)
    value_heads = value_input.astype(jnp.float32).reshape(tokens, HALF_VALUE_HEADS, DV)
    seg_flat = segments.reshape(tokens)
    position = jnp.arange(tokens, dtype=jnp.int32)
    previous = jnp.concatenate([seg_flat[:1], seg_flat[:-1]])
    keeping = jnp.where((position % TOK_DEV == 0) | (seg_flat != previous), 0.0, 1.0).astype(jnp.float32)
    factor = jnp.exp(decay_log.T) * keeping[:, None]

    def advance(memory, inputs):
        query_row, key_row, value_row, decay_row, rate_row = inputs
        recalled = jnp.einsum('hd,hde->he', key_row, memory, precision=lax.Precision.HIGHEST)
        fresh = rate_row[:, None] * (value_row - decay_row[:, None] * recalled)
        memory = decay_row[:, None, None] * memory + key_row[:, :, None] * fresh[:, None, :]
        output = jnp.einsum('hd,hde->he', query_row, memory, precision=lax.Precision.HIGHEST)
        return (memory, output)
    start_memory = jnp.zeros((HALF_VALUE_HEADS, DK, DV), jnp.float32)
    _, mixer_out = lax.scan(advance, start_memory, (query_heads, key_heads, value_heads, factor, write_rate.T))
    head_normed = mixer_out * lax.rsqrt(lax.optimization_barrier(jnp.mean(mixer_out * mixer_out, -1, keepdims=True)) + 1e-06) * head_gain
    head_normed = head_normed * jax.nn.silu(gate_input.astype(jnp.float32).reshape(tokens, HALF_VALUE_HEADS, DV))
    gated_out = head_normed.astype(jnp.bfloat16).reshape(tokens, HALF_VALUE_HEADS * DV)
    attended = jnp.dot(gated_out, out_proj, preferred_element_type=jnp.float32)
    hidden = (resid_in.astype(jnp.float32) + attended).astype(jnp.bfloat16)
    hidden_wide = hidden.astype(jnp.float32)
    normalized = hidden_wide * lax.rsqrt(lax.optimization_barrier(jnp.mean(hidden_wide * hidden_wide, -1, keepdims=True)) + 1e-06) * post_gain
    block_count = D // QBLOCK
    powers = jnp.exp2(block_exps.astype(jnp.float32))[:, :, None]
    quantized = jnp.clip(normalized.reshape(tokens, block_count, QBLOCK) / powers, -448.0, 448.0).astype(jnp.bfloat16)
    expert_in = (quantized.astype(jnp.float32) * powers).astype(jnp.bfloat16).reshape(tokens, D)
    flat_ids = route_ids.reshape(devices, TOK_DEV * TOPK)
    matches = (flat_ids[:, :, None] == jnp.arange(devices, dtype=jnp.int32)[None, None, :]).astype(jnp.int32)
    ranking = lax.optimization_barrier(jnp.sum(jnp.cumsum(matches, axis=1) * matches, axis=2)) - 1
    destination = flat_ids * (devices * CAP) + jnp.arange(devices, dtype=jnp.int32)[:, None] * CAP + ranking
    pair_count = tokens * TOPK
    table = jnp.full((devices * devices * CAP,), pair_count, jnp.int32)
    table = table.at[destination.reshape(-1)].set(jnp.arange(pair_count, dtype=jnp.int32)).reshape(devices, devices * CAP)
    rows_padded = jnp.concatenate([expert_in, jnp.zeros((1, D), jnp.bfloat16)], axis=0)
    weight_padded = jnp.concatenate([route_weights.reshape(-1), jnp.zeros((1,), jnp.float32)], axis=0)

    def expert(running, inputs):
        pair_index, gate_up, down = inputs
        token_index = pair_index // TOPK
        rows_in = rows_padded[token_index].astype(jnp.float32)
        inner = jnp.dot(rows_in, gate_up.astype(jnp.float32), preferred_element_type=jnp.float32)
        expert_hidden = (jax.nn.silu(inner[:, :FFE]) * inner[:, FFE:]).astype(jnp.bfloat16)
        projected = jnp.dot(expert_hidden.astype(jnp.float32), down.astype(jnp.float32), preferred_element_type=jnp.float32)
        expert_term = (weight_padded[pair_index][:, None] * projected).astype(jnp.bfloat16)
        running = running.at[token_index].add(expert_term.astype(jnp.float32))
        return (running, None)
    running = jnp.zeros((tokens + 1, D), jnp.float32)
    running, _ = lax.scan(expert, running, (table, w_gate_up, w_down))
    return (hidden_wide + running[:tokens]).astype(jnp.bfloat16)
```

```python
import functools

import jax
import jax.numpy as jnp
from jax import lax
from jax.experimental import pallas as pl
from jax.experimental.pallas import tpu as pltpu
from jax.sharding import PartitionSpec as P

KEY_HEADS = 8
HEAD = 128
QBLOCK = 128
LANES = 128
F32 = jnp.float32
BF16 = jnp.bfloat16
HIGHEST = lax.Precision.HIGHEST


def dot(a, b, precision=None):
    return jnp.dot(a, b, preferred_element_type=F32, precision=precision)


def dot_nt(a, b, precision=None):
    return lax.dot_general(
        a, b, (((1,), (1,)), ((), ())), preferred_element_type=F32, precision=precision
    )


def halves(a):
    high = a.astype(BF16)
    return high, (a - high.astype(F32)).astype(BF16)


def dot3(a, b):
    return dot(a[0], b[0]) + dot(a[0], b[1]) + dot(a[1], b[0])


def silu(v):
    return v / (1.0 + jnp.exp(-v))


def mixer(q_ref, k_ref, v_ref, gate_ref, decay_ref, rate_ref, seg_ref, gain_ref, gated):
    tokens = q_ref.shape[0]
    wide = 2 * tokens
    row = lax.broadcasted_iota(jnp.int32, (tokens, wide), 0)
    lane = lax.broadcasted_iota(jnp.int32, (tokens, wide), 1)
    first = lane < tokens
    col = jnp.where(first, lane, lane - tokens)
    diagonal = row == col
    eye2 = jnp.where(diagonal, 1.0, 0.0)
    upper2 = jnp.where(row <= col, 1.0, 0.0)
    r1 = lax.broadcasted_iota(jnp.int32, (tokens, tokens), 0)
    c1 = lax.broadcasted_iota(jnp.int32, (tokens, tokens), 1)
    eye1 = jnp.where(r1 == c1, 1.0, 0.0)
    lower1 = jnp.where(r1 >= c1, 1.0, 0.0)
    decay = decay_ref[...]
    cum_rows = dot(decay, upper2, HIGHEST)
    cum_cols = dot_nt(lower1, decay, HIGHEST)
    rates = dot(rate_ref[...], eye2, HIGHEST)
    segments = seg_ref[...].astype(F32)
    seg_row = dot(jnp.broadcast_to(segments, (8, tokens)), eye2, HIGHEST)[:1]
    seg_col = dot_nt(eye1, jnp.broadcast_to(segments, (8, tokens)), HIGHEST)[:, :1]
    kept = (row >= col) & (jnp.abs(seg_row - seg_col) < 0.5)
    strict = row > col
    bi = lax.broadcasted_iota(jnp.int32, (wide, wide), 0)
    bj = lax.broadcasted_iota(jnp.int32, (wide, wide), 1)
    identity = jnp.where(bi == bj, 1.0, 0.0)
    first_row = first[:1]
    gain = gain_ref[...]

    def stack(pair_matrix):
        return jnp.concatenate(
            [jnp.where(first, pair_matrix, 0.0), jnp.where(first, 0.0, pair_matrix)], axis=0
        )

    for p in range(KEY_HEADS):
        a, b = 2 * p, 2 * p + 1
        q = q_ref[:, p * HEAD : (p + 1) * HEAD]
        k = k_ref[:, p * HEAD : (p + 1) * HEAD]
        twice = jnp.concatenate([k, k], axis=0)
        kk = dot_nt(k, twice)
        qk = dot_nt(q, twice)
        own = jnp.where(diagonal, kk, 0.0)
        key_col = lax.rsqrt(jnp.sum(own, axis=1, keepdims=True) * 0.5 + 1e-06)
        key_row = lax.rsqrt(jnp.sum(own, axis=0, keepdims=True) + 1e-06)
        q_wide = q.astype(F32)
        query_col = lax.rsqrt(jnp.sum(q_wide * q_wide, axis=1, keepdims=True) + 1e-06)
        cum_col = jnp.where(first, cum_cols[:, a : a + 1], cum_cols[:, b : b + 1])
        cum_row = jnp.where(first_row, cum_rows[a : a + 1], cum_rows[b : b + 1])
        rate = jnp.where(first_row, rates[a : a + 1], rates[b : b + 1])
        decayed = jnp.where(kept, jnp.exp(jnp.where(kept, cum_col - cum_row, 0.0)), 0.0)
        weighted = decayed * (rate * key_row)
        mixing = stack(jnp.where(strict, weighted * (kk * key_col), 0.0))
        scores = stack(weighted * (qk * query_col))

        def between(level):
            return jnp.where(
                ((bi >> level) == (bj >> level)) & ((bi >> (level - 1)) != (bj >> (level - 1))),
                mixing,
                0.0,
            )

        inverse = identity - between(1)
        level = 2
        while (1 << level) <= tokens:
            split = halves(inverse)
            inner = dot3(halves(between(level)), split)
            inverse = inverse - dot3(split, halves(inner))
            level += 1
        values = jnp.concatenate(
            [v_ref[:, a * HEAD : (a + 1) * HEAD], v_ref[:, b * HEAD : (b + 1) * HEAD]], axis=0
        )
        split = halves(inverse)
        update = dot(split[0], values) + dot(split[1], values)
        mixed = dot3(halves(scores), halves(update))
        mixed = mixed * lax.rsqrt(jnp.mean(mixed * mixed, axis=1, keepdims=True) + 1e-06) * gain
        for at, head in ((0, a), (1, b)):
            gate = gate_ref[:, head * HEAD : (head + 1) * HEAD].astype(F32)
            gated[:, head * HEAD : (head + 1) * HEAD] = (
                mixed[at * tokens : (at + 1) * tokens] * silu(gate)
            ).astype(BF16)


def kernel(
    depth,
    resid_ref, q_ref, k_ref, v_ref, gate_ref, decay_ref, rate_ref, seg_ref, gain_ref,
    post_ref, exps_ref, ids_ref, weights_ref, proj_hbm, gate_up_hbm, down_hbm,
    out_ref,
    gated, proj, gate_up, down, hidden, wide_hidden, rows, terms, inner, from_b, from_a, from_z,
    load_sem, pair_send, pair_recv, ag_send, ag_recv, b_send, b_recv, a_send, a_recv, z_send, z_recv,
):
    tokens, width = resid_ref.shape
    part_rows = tokens // 2
    half = down.shape[1]
    ep = lax.axis_index("ep")
    core = lax.axis_index("sub")
    z, y, x = ep // 4, (ep // 2) % 2, ep % 2

    def at(zz, yy, xx):
        return {"ep": zz * 4 + yy * 2 + xx}

    def z_away(d):
        return lax.rem(z + d, depth)

    x_next, y_next = at(z, y, 1 - x), at(z, 1 - y, x)
    sibling = {"sub": 1 - core}
    peers = [at(z_away(d), y, x) for d in range(1, depth)] + [x_next, y_next, sibling]
    barrier = pltpu.get_barrier_semaphore()
    for peer in peers:
        pl.semaphore_signal(
            barrier, inc=1, device_id=peer, device_id_type=pl.DeviceIdType.MESH
        )
    pl.semaphore_wait(barrier, len(peers))

    def push(src, dst, send, recv, device):
        copy = pltpu.make_async_remote_copy(
            src_ref=src, dst_ref=dst, send_sem=send, recv_sem=recv,
            device_id=device, device_id_type=pl.DeviceIdType.MESH,
        )
        copy.start()
        return copy

    shared = [(proj_hbm, proj), (gate_up_hbm, gate_up), (down_hbm, down)]
    loads, swaps = [], []
    for i, (src, dst) in enumerate(shared):
        mine = dst.at[core] if i == 0 else dst.at[0]
        there = dst.at[core] if i == 0 else dst.at[1]
        swaps.append(push(src, there, pair_send.at[i], pair_recv.at[i], sibling))
        load = pltpu.make_async_copy(src, mine, load_sem.at[i])
        load.start()
        loads.append(load)

    mixer(q_ref, k_ref, v_ref, gate_ref, decay_ref, rate_ref, seg_ref, gain_ref, gated)

    loads[0].wait()
    swaps[0].wait_recv()
    tile = 512

    @pl.loop(0, width // tile)
    def _(j):
        cols = pl.ds(pl.multiple_of(j * tile, tile), tile)
        depth_half = proj.shape[1]
        total = dot(gated[:, :depth_half], proj[0, :, cols])
        total = total + dot(gated[:, depth_half:], proj[1, :, cols])
        hidden[:, cols] = (resid_ref[:, cols].astype(F32) + total).astype(BF16)

    wide_hidden[...] = hidden[...].astype(F32)
    scale = lax.rsqrt(
        jnp.mean(wide_hidden[...] * wide_hidden[...], axis=1, keepdims=True) + 1e-06
    )
    for j in range(width // QBLOCK):
        cols = slice(j * QBLOCK, (j + 1) * QBLOCK)
        exps = exps_ref[:, j : j + 1]
        power = jnp.zeros(exps.shape, F32)
        unpower = jnp.zeros(exps.shape, F32)
        for e in range(-9, -4):
            power = jnp.where(exps == e, 2.0**e, power)
            unpower = jnp.where(exps == e, 2.0**-e, unpower)
        block = wide_hidden[:, cols] * scale * post_ref[:, cols] * unpower
        block = jnp.clip(block, -448.0, 448.0).astype(BF16).astype(F32)
        block = (block * power).astype(BF16)
        for p in range(2):
            rows[y, x, z, p, :, cols] = block[p * part_rows : (p + 1) * part_rows]
    lane = lax.broadcasted_iota(jnp.int32, (tokens, LANES), 1)
    name = jnp.where(lane < LANES // 2, lane, lane - LANES // 2)
    dense = jnp.zeros((tokens, LANES), F32)
    for choice in range(ids_ref.shape[1]):
        dense = dense + jnp.where(
            name == ids_ref[:, choice : choice + 1], weights_ref[:, choice : choice + 1], 0.0
        )
    high = dense.astype(BF16).astype(F32)
    dense = jnp.where(lane < LANES // 2, high, dense - high).astype(BF16)
    for p in range(2):
        rows[y, x, z, p, :, width:] = dense[p * part_rows : (p + 1) * part_rows]

    a_next, b_next = (y_next, x_next), (x_next, y_next)
    a_col, b_col = ((1 - y, x), (y, 1 - x)), ((y, 1 - x), (1 - y, x))
    far = (1 - y, 1 - x)
    sent = []

    def gather_send(p, slot, yy, xx, zz, device):
        block = rows.at[yy, xx, zz, p]
        sent.append(
            push(block, block, ag_send.at[p, slot], ag_recv.at[p, yy * 2 + xx, zz], device)
        )

    def gather_wait(p, yy, xx, zz):
        block = rows.at[yy, xx, zz, p]
        pltpu.make_async_remote_copy(
            src_ref=block, dst_ref=block, send_sem=ag_send.at[p, 0],
            recv_sem=ag_recv.at[p, yy * 2 + xx, zz],
            device_id=x_next, device_id_type=pl.DeviceIdType.MESH,
        ).wait_recv()

    order = sorted(range(1, depth), key=lambda d: min(d, depth - d))
    for d in order:
        for p in range(2):
            gather_send(p, d - 1, y, x, z, at(z_away(d), y, x))
    base_a, base_b = depth - 1, 2 * depth - 1
    for d in [0] + order:
        for p in range(2):
            zz = z_away(d)
            if d:
                gather_wait(p, y, x, zz)
            gather_send(p, base_a + d, y, x, zz, a_next[p])
            gather_send(p, base_b + d, y, x, zz, b_next[p])

    own_expert = ep * 2 + core
    other_expert = ep * 2 + 1 - core

    def ffn(yy, xx):
        count = depth * tokens
        batch = rows[yy, xx].reshape(count, width + LANES)
        lanes = lax.broadcasted_iota(jnp.int32, (count, LANES), 1)
        shares = batch[:, width:].astype(F32)
        weight = [
            jnp.sum(
                jnp.where((lanes == e) | (lanes == e + LANES // 2), shares, 0.0),
                axis=1, keepdims=True,
            )
            for e in (own_expert, other_expert)
        ]

        @pl.loop(0, 2)
        def _(e):
            batch_in = rows[yy, xx, :, :, :, :width].reshape(count, width)
            for cut in range(half // 256):
                gate = dot(batch_in, gate_up[e, :, cut * 256 : (cut + 1) * 256])
                up = dot(batch_in, gate_up[e, :, half + cut * 256 : half + (cut + 1) * 256])
                inner[e, :, cut * 256 : (cut + 1) * 256] = (silu(gate) * up).astype(BF16)

        @pl.loop(0, width // tile)
        def _(j):
            cols = pl.ds(pl.multiple_of(j * tile, tile), tile)
            total = weight[0] * dot(inner[0], down[0, :, cols])
            total = total + weight[1] * dot(inner[1], down[1, :, cols])
            terms[yy, xx, :, :, :, cols] = total.astype(BF16).reshape(
                depth, 2, part_rows, tile
            )

    for i in (1, 2):
        loads[i].wait()
        swaps[i].wait_recv()
    ffn(y, x)

    for d in [0] + order:
        for p in range(2):
            zz = z_away(d)
            yy, xx = a_col[p]
            gather_wait(p, yy, xx, zz)
            gather_send(p, base_b + depth + d, yy, xx, zz, b_next[p])

    def b_stage(p, rel, yy, xx):
        for d in order + [0]:
            zz = z_away(d)
            sent.append(
                push(
                    terms.at[yy, xx, zz, p], from_b.at[p, rel, zz],
                    b_send.at[p, rel, zz], b_recv.at[p, rel, zz], b_next[p],
                )
            )

    for p in (0, 1):
        for d in [0] + order:
            yy, xx = b_col[p]
            gather_wait(p, yy, xx, z_away(d))
        if p == 0:
            ffn(*b_col[0])
            b_stage(0, 0, *b_col[0])
    ffn(*b_col[1])
    b_stage(1, 0, *b_col[1])
    for p in (0, 1):
        for d in [0] + order:
            gather_wait(p, far[0], far[1], z_away(d))
    ffn(*far)
    for p in (0, 1):
        b_stage(p, 1, *far)

    def arrived(buffer, recv):
        pltpu.make_async_remote_copy(
            src_ref=buffer, dst_ref=buffer, send_sem=b_send.at[0, 0, 0], recv_sem=recv,
            device_id=x_next, device_id_type=pl.DeviceIdType.MESH,
        ).wait_recv()

    for d in order + [0]:
        zz = z_away(d)
        for p in (0, 1):
            yy, xx = a_col[p]
            arrived(from_b.at[p, 1, zz], b_recv.at[p, 1, zz])
            total = terms[yy, xx, zz, p].astype(F32) + from_b[p, 1, zz].astype(F32)
            terms[yy, xx, zz, p] = total.astype(BF16)
            sent.append(
                push(
                    terms.at[yy, xx, zz, p], from_a.at[p, zz],
                    a_send.at[p, zz], a_recv.at[p, zz], a_next[p],
                )
            )
    for d in order + [0]:
        zz = z_away(d)
        for p in (0, 1):
            arrived(from_b.at[p, 0, zz], b_recv.at[p, 0, zz])
            arrived(from_a.at[p, zz], a_recv.at[p, zz])
            total = (
                terms[y, x, zz, p].astype(F32)
                + from_b[p, 0, zz].astype(F32)
                + from_a[p, zz].astype(F32)
            )
            if d:
                terms[y, x, zz, p] = total.astype(BF16)
                sent.append(
                    push(
                        terms.at[y, x, zz, p], from_z.at[p, d],
                        z_send.at[p, d], z_recv.at[p, d], at(zz, y, x),
                    )
                )
            else:
                wide_hidden[p * part_rows : (p + 1) * part_rows] = (
                    wide_hidden[p * part_rows : (p + 1) * part_rows] + total
                )
    for p in (0, 1):
        total = wide_hidden[p * part_rows : (p + 1) * part_rows]
        for d in order:
            arrived(from_z.at[p, d], z_recv.at[p, d])
            total = total + from_z[p, d].astype(F32)
        out_ref[p * part_rows : (p + 1) * part_rows] = total.astype(BF16)
    for copy in swaps + sent:
        copy.wait_send()


def per_device(
    resid_in, query_input, key_input, value_input, gate_input, decay_log, write_rate, segments,
    head_gain, out_proj, post_gain, block_exps, route_ids, route_weights, w_gate_up, w_down,
):
    tokens, width = resid_in.shape
    depth = lax.axis_size("ep") // 4
    part = tokens // 2
    hidden_units = w_down.shape[1]
    vmem = pl.BlockSpec(memory_space=pltpu.VMEM)
    hbm = pl.BlockSpec(memory_space=pl.ANY)
    dma = pltpu.SemaphoreType.DMA
    return pl.pallas_call(
        functools.partial(kernel, depth),
        out_shape=jax.ShapeDtypeStruct((tokens, width), BF16),
        in_specs=[vmem] * 13 + [hbm] * 3,
        out_specs=vmem,
        scratch_shapes=[
            pltpu.VMEM((tokens, width), BF16),
            pltpu.VMEM((2,) + out_proj.shape, BF16),
            pltpu.VMEM((2,) + w_gate_up.shape[1:], BF16),
            pltpu.VMEM((2,) + w_down.shape[1:], BF16),
            pltpu.VMEM((tokens, width), BF16),
            pltpu.VMEM((tokens, width), F32),
            pltpu.VMEM((2, 2, depth, 2, part, width + LANES), BF16),
            pltpu.VMEM((2, 2, depth, 2, part, width), BF16),
            pltpu.VMEM((2, depth * tokens, hidden_units), BF16),
            pltpu.VMEM((2, 2, depth, part, width), BF16),
            pltpu.VMEM((2, depth, part, width), BF16),
            pltpu.VMEM((2, depth, part, width), BF16),
            dma((3,)), dma((3,)), dma((3,)),
            dma((2, 4 * depth - 1)), dma((2, 4, depth)),
            dma((2, 2, depth)), dma((2, 2, depth)),
            dma((2, depth)), dma((2, depth)),
            dma((2, depth)), dma((2, depth)),
        ],
        compiler_params=pltpu.CompilerParams(
            collective_id=0, has_side_effects=True, vmem_limit_bytes=60 * 1024 * 1024
        ),
        cost_estimate=pl.CostEstimate(
            flops=14_000_000_000, bytes_accessed=24_000_000, transcendentals=2_000_000
        ),
    )(
        resid_in, query_input, key_input, value_input, gate_input, decay_log, write_rate, segments,
        head_gain.reshape(1, -1), post_gain.reshape(1, -1), block_exps, route_ids, route_weights,
        out_proj, w_gate_up[0], w_down[0],
    )


def solution(mesh):
    rows = P(("grp", "ep", "sub"), None)
    return jax.shard_map(
        per_device,
        mesh=mesh,
        in_specs=(
            rows, rows, rows, rows, rows,
            P(None, ("grp", "ep", "sub")),
            P(None, ("grp", "ep", "sub")),
            rows,
            P(),
            P("sub", None),
            P(),
            rows, rows, rows,
            P(("ep", "sub"), None, None),
            P(("ep", "sub"), None, None),
        ),
        out_specs=rows,
        check_vma=False,
    )
```

```python
import functools

import jax
import jax.numpy as jnp
from jax import lax
from jax.experimental import pallas as pl
from jax.experimental.pallas import tpu as pltpu
from jax.sharding import PartitionSpec as P

KEY_HEADS = 8
HEAD = 128
QBLOCK = 128
LANES = 128
F32 = jnp.float32
BF16 = jnp.bfloat16
HIGHEST = lax.Precision.HIGHEST


def dot(a, b, precision=None):
    return jnp.dot(a, b, preferred_element_type=F32, precision=precision)


def dot_nt(a, b, precision=None):
    return lax.dot_general(
        a, b, (((1,), (1,)), ((), ())), preferred_element_type=F32, precision=precision
    )


def halves(a):
    high = a.astype(BF16)
    return high, (a - high.astype(F32)).astype(BF16)


def dot3(a, b):
    return dot(a[0], b[0]) + dot(a[0], b[1]) + dot(a[1], b[0])


def silu(v):
    return v / (1.0 + jnp.exp(-v))


def mixer(q_ref, k_ref, v_ref, gate_ref, decay_ref, rate_ref, seg_ref, gain_ref, gated):
    tokens = q_ref.shape[0]
    wide = 2 * tokens
    row = lax.broadcasted_iota(jnp.int32, (tokens, wide), 0)
    lane = lax.broadcasted_iota(jnp.int32, (tokens, wide), 1)
    first = lane < tokens
    col = jnp.where(first, lane, lane - tokens)
    diagonal = row == col
    eye2 = jnp.where(diagonal, 1.0, 0.0)
    upper2 = jnp.where(row <= col, 1.0, 0.0)
    r1 = lax.broadcasted_iota(jnp.int32, (tokens, tokens), 0)
    c1 = lax.broadcasted_iota(jnp.int32, (tokens, tokens), 1)
    eye1 = jnp.where(r1 == c1, 1.0, 0.0)
    lower1 = jnp.where(r1 >= c1, 1.0, 0.0)
    decay = decay_ref[...]
    cum_rows = dot(decay, upper2, HIGHEST)
    cum_cols = dot_nt(lower1, decay, HIGHEST)
    rates = dot(rate_ref[...], eye2, HIGHEST)
    segments = seg_ref[...].astype(F32)
    seg_row = dot(jnp.broadcast_to(segments, (8, tokens)), eye2, HIGHEST)[:1]
    seg_col = dot_nt(eye1, jnp.broadcast_to(segments, (8, tokens)), HIGHEST)[:, :1]
    kept = (row >= col) & (jnp.abs(seg_row - seg_col) < 0.5)
    strict = row > col
    bi = lax.broadcasted_iota(jnp.int32, (wide, wide), 0)
    bj = lax.broadcasted_iota(jnp.int32, (wide, wide), 1)
    identity = jnp.where(bi == bj, 1.0, 0.0)
    first_row = first[:1]
    gain = gain_ref[...]

    def stack(pair_matrix):
        return jnp.concatenate(
            [jnp.where(first, pair_matrix, 0.0), jnp.where(first, 0.0, pair_matrix)], axis=0
        )

    for p in range(KEY_HEADS):
        a, b = 2 * p, 2 * p + 1
        q = q_ref[:, p * HEAD : (p + 1) * HEAD]
        k = k_ref[:, p * HEAD : (p + 1) * HEAD]
        twice = jnp.concatenate([k, k], axis=0)
        kk = dot_nt(k, twice)
        qk = dot_nt(q, twice)
        own = jnp.where(diagonal, kk, 0.0)
        key_col = lax.rsqrt(jnp.sum(own, axis=1, keepdims=True) * 0.5 + 1e-06)
        key_row = lax.rsqrt(jnp.sum(own, axis=0, keepdims=True) + 1e-06)
        q_wide = q.astype(F32)
        query_col = lax.rsqrt(jnp.sum(q_wide * q_wide, axis=1, keepdims=True) + 1e-06)
        cum_col = jnp.where(first, cum_cols[:, a : a + 1], cum_cols[:, b : b + 1])
        cum_row = jnp.where(first_row, cum_rows[a : a + 1], cum_rows[b : b + 1])
        rate = jnp.where(first_row, rates[a : a + 1], rates[b : b + 1])
        decayed = jnp.where(kept, jnp.exp(jnp.where(kept, cum_col - cum_row, 0.0)), 0.0)
        weighted = decayed * (rate * key_row)
        mixing = stack(jnp.where(strict, weighted * (kk * key_col), 0.0))
        scores = stack(weighted * (qk * query_col))

        def between(level):
            return jnp.where(
                ((bi >> level) == (bj >> level)) & ((bi >> (level - 1)) != (bj >> (level - 1))),
                mixing,
                0.0,
            )

        inverse = identity - between(1)
        level = 2
        while (1 << level) <= tokens:
            split = halves(inverse)
            inner = dot3(halves(between(level)), split)
            inverse = inverse - dot3(split, halves(inner))
            level += 1
        values = jnp.concatenate(
            [v_ref[:, a * HEAD : (a + 1) * HEAD], v_ref[:, b * HEAD : (b + 1) * HEAD]], axis=0
        )
        split = halves(inverse)
        update = dot(split[0], values) + dot(split[1], values)
        mixed = dot3(halves(scores), halves(update))
        mixed = mixed * lax.rsqrt(jnp.mean(mixed * mixed, axis=1, keepdims=True) + 1e-06) * gain
        for at, head in ((0, a), (1, b)):
            gate = gate_ref[:, head * HEAD : (head + 1) * HEAD].astype(F32)
            gated[:, head * HEAD : (head + 1) * HEAD] = (
                mixed[at * tokens : (at + 1) * tokens] * silu(gate)
            ).astype(BF16)


def kernel(
    depth,
    resid_ref, q_ref, k_ref, v_ref, gate_ref, decay_ref, rate_ref, seg_ref, gain_ref,
    post_ref, exps_ref, ids_ref, weights_ref, proj_hbm, gate_up_hbm, down_hbm,
    out_ref,
    gated, proj, gate_up, down, hidden, wide_hidden, rows, terms, inner, from_b, from_a, from_z,
    load_sem, pair_send, pair_recv, ag_send, ag_recv, b_send, b_recv, a_send, a_recv, z_send, z_recv,
):
    tokens, width = resid_ref.shape
    part_rows = tokens // 2
    half = down.shape[1]
    ep = lax.axis_index("ep")
    core = lax.axis_index("sub")
    z, y, x = ep // 4, (ep // 2) % 2, ep % 2

    def at(zz, yy, xx):
        return {"ep": zz * 4 + yy * 2 + xx}

    def z_away(d):
        return lax.rem(z + d, depth)

    x_next, y_next = at(z, y, 1 - x), at(z, 1 - y, x)
    sibling = {"sub": 1 - core}
    peers = [at(z_away(d), y, x) for d in range(1, depth)] + [x_next, y_next, sibling]
    barrier = pltpu.get_barrier_semaphore()
    for peer in peers:
        pl.semaphore_signal(
            barrier, inc=1, device_id=peer, device_id_type=pl.DeviceIdType.MESH
        )
    pl.semaphore_wait(barrier, len(peers))

    def push(src, dst, send, recv, device):
        copy = pltpu.make_async_remote_copy(
            src_ref=src, dst_ref=dst, send_sem=send, recv_sem=recv,
            device_id=device, device_id_type=pl.DeviceIdType.MESH,
        )
        copy.start()
        return copy

    shared = [(proj_hbm, proj), (gate_up_hbm, gate_up), (down_hbm, down)]
    loads, swaps = [], []
    for i, (src, dst) in enumerate(shared):
        mine = dst.at[core] if i == 0 else dst.at[0]
        there = dst.at[core] if i == 0 else dst.at[1]
        swaps.append(push(src, there, pair_send.at[i], pair_recv.at[i], sibling))
        load = pltpu.make_async_copy(src, mine, load_sem.at[i])
        load.start()
        loads.append(load)

    mixer(q_ref, k_ref, v_ref, gate_ref, decay_ref, rate_ref, seg_ref, gain_ref, gated)

    loads[0].wait()
    swaps[0].wait_recv()
    tile = 512

    @pl.loop(0, width // tile)
    def _(j):
        cols = pl.ds(pl.multiple_of(j * tile, tile), tile)
        depth_half = proj.shape[1]
        total = dot(gated[:, :depth_half], proj[0, :, cols])
        total = total + dot(gated[:, depth_half:], proj[1, :, cols])
        hidden[:, cols] = (resid_ref[:, cols].astype(F32) + total).astype(BF16)

    wide_hidden[...] = hidden[...].astype(F32)
    scale = lax.rsqrt(
        jnp.mean(wide_hidden[...] * wide_hidden[...], axis=1, keepdims=True) + 1e-06
    )
    r1 = lax.broadcasted_iota(jnp.int32, (tokens, tokens), 0)
    c1 = lax.broadcasted_iota(jnp.int32, (tokens, tokens), 1)
    eye = jnp.where(r1 == c1, 1.0, 0.0)
    all_exps = dot_nt(eye, exps_ref[...].astype(F32), HIGHEST)
    ids = dot_nt(eye, ids_ref[...].astype(F32), HIGHEST)
    weights = dot_nt(eye, weights_ref[...], HIGHEST)
    for j in range(width // QBLOCK):
        cols = slice(j * QBLOCK, (j + 1) * QBLOCK)
        exps = all_exps[:, j : j + 1]
        power = jnp.zeros(exps.shape, F32)
        unpower = jnp.zeros(exps.shape, F32)
        for e in range(-9, -4):
            power = jnp.where(exps == e, 2.0**e, power)
            unpower = jnp.where(exps == e, 2.0**-e, unpower)
        block = wide_hidden[:, cols] * scale * post_ref[:, cols] * unpower
        block = jnp.clip(block, -448.0, 448.0).astype(BF16).astype(F32)
        block = (block * power).astype(BF16)
        for p in range(2):
            rows[y, x, z, p, :, cols] = block[p * part_rows : (p + 1) * part_rows]
    lane = lax.broadcasted_iota(jnp.int32, (tokens, LANES), 1)
    name = jnp.where(lane < LANES // 2, lane, lane - LANES // 2).astype(F32)
    dense = jnp.zeros((tokens, LANES), F32)
    for choice in range(ids_ref.shape[0]):
        dense = dense + jnp.where(
            name == ids[:, choice : choice + 1], weights[:, choice : choice + 1], 0.0
        )
    high = dense.astype(BF16).astype(F32)
    dense = jnp.where(lane < LANES // 2, high, dense - high).astype(BF16)
    for p in range(2):
        rows[y, x, z, p, :, width:] = dense[p * part_rows : (p + 1) * part_rows]

    a_next, b_next = (y_next, x_next), (x_next, y_next)
    a_col, b_col = ((1 - y, x), (y, 1 - x)), ((y, 1 - x), (1 - y, x))
    far = (1 - y, 1 - x)
    sent = []

    def gather_send(p, slot, yy, xx, zz, device):
        block = rows.at[yy, xx, zz, p]
        sent.append(
            push(block, block, ag_send.at[p, slot], ag_recv.at[p, yy * 2 + xx, zz], device)
        )

    def gather_wait(p, yy, xx, zz):
        block = rows.at[yy, xx, zz, p]
        pltpu.make_async_remote_copy(
            src_ref=block, dst_ref=block, send_sem=ag_send.at[p, 0],
            recv_sem=ag_recv.at[p, yy * 2 + xx, zz],
            device_id=x_next, device_id_type=pl.DeviceIdType.MESH,
        ).wait_recv()

    order = sorted(range(1, depth), key=lambda d: min(d, depth - d))
    for d in order:
        for p in range(2):
            gather_send(p, d - 1, y, x, z, at(z_away(d), y, x))
    base_a, base_b = depth - 1, 2 * depth - 1

    def along_z(d):
        for p in range(2):
            zz = z_away(d)
            if d:
                gather_wait(p, y, x, zz)
            gather_send(p, base_a + d, y, x, zz, a_next[p])
            gather_send(p, base_b + d, y, x, zz, b_next[p])

    def along_a(d):
        for p in range(2):
            zz = z_away(d)
            yy, xx = a_col[p]
            gather_wait(p, yy, xx, zz)
            gather_send(p, base_b + depth + d, yy, xx, zz, b_next[p])

    along_z(0)
    along_a(0)
    for i, d in enumerate(order):
        along_z(d)
        if i:
            along_a(order[i - 1])
    along_a(order[-1])

    own_expert = ep * 2 + core
    other_expert = ep * 2 + 1 - core

    def ffn(yy, xx):
        count = depth * tokens
        batch = rows[yy, xx].reshape(count, width + LANES)
        lanes = lax.broadcasted_iota(jnp.int32, (count, LANES), 1)
        shares = batch[:, width:].astype(F32)
        weight = [
            jnp.sum(
                jnp.where((lanes == e) | (lanes == e + LANES // 2), shares, 0.0),
                axis=1, keepdims=True,
            )
            for e in (own_expert, other_expert)
        ]

        @pl.loop(0, 2)
        def _(e):
            batch_in = rows[yy, xx, :, :, :, :width].reshape(count, width)
            for cut in range(half // 256):
                gate = dot(batch_in, gate_up[e, :, cut * 256 : (cut + 1) * 256])
                up = dot(batch_in, gate_up[e, :, half + cut * 256 : half + (cut + 1) * 256])
                inner[e, :, cut * 256 : (cut + 1) * 256] = (silu(gate) * up).astype(BF16)

        @pl.loop(0, width // tile)
        def _(j):
            cols = pl.ds(pl.multiple_of(j * tile, tile), tile)
            total = weight[0] * dot(inner[0], down[0, :, cols])
            total = total + weight[1] * dot(inner[1], down[1, :, cols])
            terms[yy, xx, :, :, :, cols] = total.astype(BF16).reshape(
                depth, 2, part_rows, tile
            )

    for i in (1, 2):
        loads[i].wait()
        swaps[i].wait_recv()
    ffn(y, x)

    back = order[::-1] + [0]

    def b_stage(p, rel, yy, xx):
        for d in back:
            zz = z_away(d)
            sent.append(
                push(
                    terms.at[yy, xx, zz, p], from_b.at[p, rel, zz],
                    b_send.at[p, rel, zz], b_recv.at[p, rel, zz], b_next[p],
                )
            )

    for p in (0, 1):
        for d in [0] + order:
            yy, xx = b_col[p]
            gather_wait(p, yy, xx, z_away(d))
        if p == 0:
            ffn(*b_col[0])
            b_stage(0, 0, *b_col[0])
    ffn(*b_col[1])
    b_stage(1, 0, *b_col[1])
    for p in (0, 1):
        for d in [0] + order:
            gather_wait(p, far[0], far[1], z_away(d))
    ffn(*far)
    for p in (0, 1):
        b_stage(p, 1, *far)

    def arrived(buffer, recv):
        pltpu.make_async_remote_copy(
            src_ref=buffer, dst_ref=buffer, send_sem=b_send.at[0, 0, 0], recv_sem=recv,
            device_id=x_next, device_id_type=pl.DeviceIdType.MESH,
        ).wait_recv()

    def reduce_a(d):
        zz = z_away(d)
        for p in (0, 1):
            yy, xx = a_col[p]
            arrived(from_b.at[p, 1, zz], b_recv.at[p, 1, zz])
            total = terms[yy, xx, zz, p].astype(F32) + from_b[p, 1, zz].astype(F32)
            terms[yy, xx, zz, p] = total.astype(BF16)
            sent.append(
                push(
                    terms.at[yy, xx, zz, p], from_a.at[p, zz],
                    a_send.at[p, zz], a_recv.at[p, zz], a_next[p],
                )
            )

    def reduce_z(d):
        zz = z_away(d)
        for p in (0, 1):
            arrived(from_b.at[p, 0, zz], b_recv.at[p, 0, zz])
            arrived(from_a.at[p, zz], a_recv.at[p, zz])
            total = (
                terms[y, x, zz, p].astype(F32)
                + from_b[p, 0, zz].astype(F32)
                + from_a[p, zz].astype(F32)
            )
            if d:
                terms[y, x, zz, p] = total.astype(BF16)
                sent.append(
                    push(
                        terms.at[y, x, zz, p], from_z.at[p, d],
                        z_send.at[p, d], z_recv.at[p, d], at(zz, y, x),
                    )
                )
            else:
                wide_hidden[p * part_rows : (p + 1) * part_rows] = (
                    wide_hidden[p * part_rows : (p + 1) * part_rows] + total
                )

    for i, d in enumerate(back):
        reduce_a(d)
        if i:
            reduce_z(back[i - 1])
    reduce_z(back[-1])
    for p in (0, 1):
        total = wide_hidden[p * part_rows : (p + 1) * part_rows]
        for d in order:
            arrived(from_z.at[p, d], z_recv.at[p, d])
            total = total + from_z[p, d].astype(F32)
        out_ref[p * part_rows : (p + 1) * part_rows] = total.astype(BF16)
    for copy in swaps + sent:
        copy.wait_send()


def per_device(
    resid_in, query_input, key_input, value_input, gate_input, decay_log, write_rate, segments,
    head_gain, out_proj, post_gain, block_exps, route_ids, route_weights, w_gate_up, w_down,
):
    tokens, width = resid_in.shape
    depth = lax.axis_size("ep") // 4
    part = tokens // 2
    hidden_units = w_down.shape[1]
    vmem = pl.BlockSpec(memory_space=pltpu.VMEM)
    hbm = pl.BlockSpec(memory_space=pl.ANY)
    dma = pltpu.SemaphoreType.DMA
    return pl.pallas_call(
        functools.partial(kernel, depth),
        out_shape=jax.ShapeDtypeStruct((tokens, width), BF16),
        in_specs=[vmem] * 13 + [hbm] * 3,
        out_specs=vmem,
        scratch_shapes=[
            pltpu.VMEM((tokens, width), BF16),
            pltpu.VMEM((2,) + out_proj.shape, BF16),
            pltpu.VMEM((2,) + w_gate_up.shape[1:], BF16),
            pltpu.VMEM((2,) + w_down.shape[1:], BF16),
            pltpu.VMEM((tokens, width), BF16),
            pltpu.VMEM((tokens, width), F32),
            pltpu.VMEM((2, 2, depth, 2, part, width + LANES), BF16),
            pltpu.VMEM((2, 2, depth, 2, part, width), BF16),
            pltpu.VMEM((2, depth * tokens, hidden_units), BF16),
            pltpu.VMEM((2, 2, depth, part, width), BF16),
            pltpu.VMEM((2, depth, part, width), BF16),
            pltpu.VMEM((2, depth, part, width), BF16),
            dma((3,)), dma((3,)), dma((3,)),
            dma((2, 4 * depth - 1)), dma((2, 4, depth)),
            dma((2, 2, depth)), dma((2, 2, depth)),
            dma((2, depth)), dma((2, depth)),
            dma((2, depth)), dma((2, depth)),
        ],
        compiler_params=pltpu.CompilerParams(
            collective_id=0, has_side_effects=True, vmem_limit_bytes=60 * 1024 * 1024
        ),
        cost_estimate=pl.CostEstimate(
            flops=14_000_000_000, bytes_accessed=24_000_000, transcendentals=2_000_000
        ),
    )(
        resid_in, query_input, key_input, value_input, gate_input, decay_log, write_rate, segments,
        head_gain.reshape(1, -1), post_gain.reshape(1, -1), block_exps.T, route_ids.T, route_weights.T,
        out_proj, w_gate_up[0], w_down[0],
    )


def solution(mesh):
    rows = P(("grp", "ep", "sub"), None)
    return jax.shard_map(
        per_device,
        mesh=mesh,
        in_specs=(
            rows, rows, rows, rows, rows,
            P(None, ("grp", "ep", "sub")),
            P(None, ("grp", "ep", "sub")),
            rows,
            P(),
            P("sub", None),
            P(),
            rows, rows, rows,
            P(("ep", "sub"), None, None),
            P(("ep", "sub"), None, None),
        ),
        out_specs=rows,
        check_vma=False,
    )
```

```python
import functools

import jax
import jax.numpy as jnp
from jax import lax
from jax.experimental import pallas as pl
from jax.experimental.pallas import tpu as pltpu
from jax.sharding import PartitionSpec as P

KEY_HEADS = 8
HEAD = 128
QBLOCK = 128
LANES = 128
F32 = jnp.float32
BF16 = jnp.bfloat16
HIGHEST = lax.Precision.HIGHEST


def dot(a, b, precision=None):
    return jnp.dot(a, b, preferred_element_type=F32, precision=precision)


def dot_nt(a, b, precision=None):
    return lax.dot_general(
        a, b, (((1,), (1,)), ((), ())), preferred_element_type=F32, precision=precision
    )


def halves(a):
    high = a.astype(BF16)
    return high, (a - high.astype(F32)).astype(BF16)


def dot3(a, b):
    return dot(a[0], b[0]) + dot(a[0], b[1]) + dot(a[1], b[0])


def silu(v):
    return v / (1.0 + jnp.exp(-v))


def mixer(q_ref, k_ref, v_ref, gate_ref, decay_ref, rate_ref, seg_ref, gain_ref, gated):
    tokens = q_ref.shape[0]
    wide = 2 * tokens
    row = lax.broadcasted_iota(jnp.int32, (tokens, wide), 0)
    lane = lax.broadcasted_iota(jnp.int32, (tokens, wide), 1)
    first = lane < tokens
    col = jnp.where(first, lane, lane - tokens)
    diagonal = row == col
    eye2 = jnp.where(diagonal, 1.0, 0.0)
    upper2 = jnp.where(row <= col, 1.0, 0.0)
    r1 = lax.broadcasted_iota(jnp.int32, (tokens, tokens), 0)
    c1 = lax.broadcasted_iota(jnp.int32, (tokens, tokens), 1)
    eye1 = jnp.where(r1 == c1, 1.0, 0.0)
    lower1 = jnp.where(r1 >= c1, 1.0, 0.0)
    decay = decay_ref[...]
    cum_rows = dot(decay, upper2, HIGHEST)
    cum_cols = dot_nt(lower1, decay, HIGHEST)
    rates = dot(rate_ref[...], eye2, HIGHEST)
    segments = seg_ref[...].astype(F32)
    seg_row = dot(jnp.broadcast_to(segments, (8, tokens)), eye2, HIGHEST)[:1]
    seg_col = dot_nt(eye1, jnp.broadcast_to(segments, (8, tokens)), HIGHEST)[:, :1]
    kept = (row >= col) & (jnp.abs(seg_row - seg_col) < 0.5)
    strict = row > col
    bi = lax.broadcasted_iota(jnp.int32, (wide, wide), 0)
    bj = lax.broadcasted_iota(jnp.int32, (wide, wide), 1)
    identity = jnp.where(bi == bj, 1.0, 0.0)
    first_row = first[:1]
    gain = gain_ref[...]

    def stack(pair_matrix):
        return jnp.concatenate(
            [jnp.where(first, pair_matrix, 0.0), jnp.where(first, 0.0, pair_matrix)], axis=0
        )

    for p in range(KEY_HEADS):
        a, b = 2 * p, 2 * p + 1
        q = q_ref[:, p * HEAD : (p + 1) * HEAD]
        k = k_ref[:, p * HEAD : (p + 1) * HEAD]
        twice = jnp.concatenate([k, k], axis=0)
        kk = dot_nt(k, twice)
        qk = dot_nt(q, twice)
        own = jnp.where(diagonal, kk, 0.0)
        key_col = lax.rsqrt(jnp.sum(own, axis=1, keepdims=True) * 0.5 + 1e-06)
        key_row = lax.rsqrt(jnp.sum(own, axis=0, keepdims=True) + 1e-06)
        q_wide = q.astype(F32)
        query_col = lax.rsqrt(jnp.sum(q_wide * q_wide, axis=1, keepdims=True) + 1e-06)
        cum_col = jnp.where(first, cum_cols[:, a : a + 1], cum_cols[:, b : b + 1])
        cum_row = jnp.where(first_row, cum_rows[a : a + 1], cum_rows[b : b + 1])
        rate = jnp.where(first_row, rates[a : a + 1], rates[b : b + 1])
        decayed = jnp.where(kept, jnp.exp(jnp.where(kept, cum_col - cum_row, 0.0)), 0.0)
        weighted = decayed * (rate * key_row)
        mixing = stack(jnp.where(strict, weighted * (kk * key_col), 0.0))
        scores = stack(weighted * (qk * query_col))

        def between(level):
            return jnp.where(
                ((bi >> level) == (bj >> level)) & ((bi >> (level - 1)) != (bj >> (level - 1))),
                mixing,
                0.0,
            )

        inverse = identity - between(1)
        level = 2
        while (1 << level) <= tokens:
            split = halves(inverse)
            inner = dot3(halves(between(level)), split)
            inverse = inverse - dot3(split, halves(inner))
            level += 1
        values = jnp.concatenate(
            [v_ref[:, a * HEAD : (a + 1) * HEAD], v_ref[:, b * HEAD : (b + 1) * HEAD]], axis=0
        )
        split = halves(inverse)
        update = dot(split[0], values) + dot(split[1], values)
        mixed = dot3(halves(scores), halves(update))
        mixed = mixed * lax.rsqrt(jnp.mean(mixed * mixed, axis=1, keepdims=True) + 1e-06) * gain
        for at, head in ((0, a), (1, b)):
            gate = gate_ref[:, head * HEAD : (head + 1) * HEAD].astype(F32)
            gated[:, head * HEAD : (head + 1) * HEAD] = (
                mixed[at * tokens : (at + 1) * tokens] * silu(gate)
            ).astype(BF16)


def kernel(
    depth,
    resid_ref, q_ref, k_ref, v_ref, gate_ref, decay_ref, rate_ref, seg_ref, gain_ref,
    post_ref, exps_ref, ids_ref, weights_ref, proj_hbm, gate_up_hbm, down_hbm,
    out_ref,
    gated, proj, gate_up, down, hidden, wide_hidden, rows, terms, inner, from_b, from_a, from_z,
    load_sem, pair_send, pair_recv, ag_send, ag_recv, b_send, b_recv, a_send, a_recv, z_send, z_recv,
):
    tokens, width = resid_ref.shape
    part_rows = tokens // 2
    half = down.shape[1]
    ep = lax.axis_index("ep")
    core = lax.axis_index("sub")
    z, y, x = ep // 4, (ep // 2) % 2, ep % 2

    def at(zz, yy, xx):
        return {"ep": zz * 4 + yy * 2 + xx}

    def z_away(d):
        return lax.rem(z + d, depth)

    x_next, y_next = at(z, y, 1 - x), at(z, 1 - y, x)
    sibling = {"sub": 1 - core}
    peers = [at(z_away(d), y, x) for d in range(1, depth)] + [x_next, y_next, sibling]
    barrier = pltpu.get_barrier_semaphore()
    for peer in peers:
        pl.semaphore_signal(
            barrier, inc=1, device_id=peer, device_id_type=pl.DeviceIdType.MESH
        )
    pl.semaphore_wait(barrier, len(peers))

    def push(src, dst, send, recv, device):
        copy = pltpu.make_async_remote_copy(
            src_ref=src, dst_ref=dst, send_sem=send, recv_sem=recv,
            device_id=device, device_id_type=pl.DeviceIdType.MESH,
        )
        copy.start()
        return copy

    shared = [(proj_hbm, proj), (gate_up_hbm, gate_up), (down_hbm, down)]
    loads, swaps = [], []
    for i, (src, dst) in enumerate(shared):
        mine = dst.at[core] if i == 0 else dst.at[0]
        there = dst.at[core] if i == 0 else dst.at[1]
        swaps.append(push(src, there, pair_send.at[i], pair_recv.at[i], sibling))
        load = pltpu.make_async_copy(src, mine, load_sem.at[i])
        load.start()
        loads.append(load)

    mixer(q_ref, k_ref, v_ref, gate_ref, decay_ref, rate_ref, seg_ref, gain_ref, gated)

    loads[0].wait()
    swaps[0].wait_recv()
    tile = 512

    @pl.loop(0, width // tile)
    def _(j):
        cols = pl.ds(pl.multiple_of(j * tile, tile), tile)
        depth_half = proj.shape[1]
        total = dot(gated[:, :depth_half], proj[0, :, cols])
        total = total + dot(gated[:, depth_half:], proj[1, :, cols])
        hidden[:, cols] = (resid_ref[:, cols].astype(F32) + total).astype(BF16)

    wide_hidden[...] = hidden[...].astype(F32)
    scale = lax.rsqrt(
        jnp.mean(wide_hidden[...] * wide_hidden[...], axis=1, keepdims=True) + 1e-06
    )
    r1 = lax.broadcasted_iota(jnp.int32, (tokens, tokens), 0)
    c1 = lax.broadcasted_iota(jnp.int32, (tokens, tokens), 1)
    eye = jnp.where(r1 == c1, 1.0, 0.0)
    all_exps = dot_nt(eye, exps_ref[...].astype(F32), HIGHEST)
    ids = dot_nt(eye, ids_ref[...].astype(F32), HIGHEST)
    weights = dot_nt(eye, weights_ref[...], HIGHEST)
    for j in range(width // QBLOCK):
        cols = slice(j * QBLOCK, (j + 1) * QBLOCK)
        exps = all_exps[:, j : j + 1]
        power = jnp.zeros(exps.shape, F32)
        unpower = jnp.zeros(exps.shape, F32)
        for e in range(-9, -4):
            power = jnp.where(exps == e, 2.0**e, power)
            unpower = jnp.where(exps == e, 2.0**-e, unpower)
        block = wide_hidden[:, cols] * scale * post_ref[:, cols] * unpower
        block = jnp.clip(block, -448.0, 448.0).astype(BF16).astype(F32)
        block = (block * power).astype(BF16)
        for p in range(2):
            rows[y, x, z, p, :, cols] = block[p * part_rows : (p + 1) * part_rows]
    lane = lax.broadcasted_iota(jnp.int32, (tokens, LANES), 1)
    name = jnp.where(lane < LANES // 2, lane, lane - LANES // 2).astype(F32)
    dense = jnp.zeros((tokens, LANES), F32)
    for choice in range(ids_ref.shape[0]):
        dense = dense + jnp.where(
            name == ids[:, choice : choice + 1], weights[:, choice : choice + 1], 0.0
        )
    high = dense.astype(BF16).astype(F32)
    dense = jnp.where(lane < LANES // 2, high, dense - high).astype(BF16)
    for p in range(2):
        rows[y, x, z, p, :, width:] = dense[p * part_rows : (p + 1) * part_rows]

    a_next, b_next = (y_next, x_next), (x_next, y_next)
    a_col, b_col = ((1 - y, x), (y, 1 - x)), ((y, 1 - x), (1 - y, x))
    far = (1 - y, 1 - x)
    sent = []

    def gather_send(p, slot, yy, xx, zz, device):
        block = rows.at[yy, xx, zz, p]
        sent.append(
            push(block, block, ag_send.at[p, slot], ag_recv.at[p, yy * 2 + xx, zz], device)
        )

    def gather_wait(p, yy, xx, zz):
        block = rows.at[yy, xx, zz, p]
        pltpu.make_async_remote_copy(
            src_ref=block, dst_ref=block, send_sem=ag_send.at[p, 0],
            recv_sem=ag_recv.at[p, yy * 2 + xx, zz],
            device_id=x_next, device_id_type=pl.DeviceIdType.MESH,
        ).wait_recv()

    order = sorted(range(1, depth), key=lambda d: min(d, depth - d))
    for d in order:
        for p in range(2):
            gather_send(p, d - 1, y, x, z, at(z_away(d), y, x))
    base_a, base_b = depth - 1, 2 * depth - 1

    def along_z(d):
        for p in range(2):
            zz = z_away(d)
            if d:
                gather_wait(p, y, x, zz)
            gather_send(p, base_a + d, y, x, zz, a_next[p])
            gather_send(p, base_b + d, y, x, zz, b_next[p])

    def along_a(d):
        for p in range(2):
            zz = z_away(d)
            yy, xx = a_col[p]
            gather_wait(p, yy, xx, zz)
            gather_send(p, base_b + depth + d, yy, xx, zz, b_next[p])

    along_z(0)
    along_a(0)
    for i, d in enumerate(order):
        along_z(d)
        if i:
            along_a(order[i - 1])
    along_a(order[-1])

    own_expert = ep * 2 + core
    other_expert = ep * 2 + 1 - core

    def ffn(yy, xx):
        count = depth * tokens
        batch = rows[yy, xx].reshape(count, width + LANES)
        lanes = lax.broadcasted_iota(jnp.int32, (count, LANES), 1)
        shares = batch[:, width:].astype(F32)
        weight = [
            jnp.sum(
                jnp.where((lanes == e) | (lanes == e + LANES // 2), shares, 0.0),
                axis=1, keepdims=True,
            )
            for e in (own_expert, other_expert)
        ]

        @pl.loop(0, 2)
        def _(e):
            batch_in = rows[yy, xx, :, :, :, :width].reshape(count, width)
            for cut in range(half // 256):
                gate = dot(batch_in, gate_up[e, :, cut * 256 : (cut + 1) * 256])
                up = dot(batch_in, gate_up[e, :, half + cut * 256 : half + (cut + 1) * 256])
                inner[e, :, cut * 256 : (cut + 1) * 256] = (silu(gate) * up).astype(BF16)

        @pl.loop(0, width // tile)
        def _(j):
            cols = pl.ds(pl.multiple_of(j * tile, tile), tile)
            total = weight[0] * dot(inner[0], down[0, :, cols])
            total = total + weight[1] * dot(inner[1], down[1, :, cols])
            terms[yy, xx, :, :, :, cols] = total.astype(BF16).reshape(
                depth, 2, part_rows, tile
            )

    for i in (1, 2):
        loads[i].wait()
        swaps[i].wait_recv()
    ffn(y, x)

    back = order[::-1] + [0]

    def b_stage(p, rel, yy, xx, which):
        for d in which:
            zz = z_away(d)
            sent.append(
                push(
                    terms.at[yy, xx, zz, p], from_b.at[p, rel, zz],
                    b_send.at[p, rel, zz], b_recv.at[p, rel, zz], b_next[p],
                )
            )

    for p in (0, 1):
        for d in [0] + order:
            yy, xx = b_col[p]
            gather_wait(p, yy, xx, z_away(d))
        if p == 0:
            ffn(*b_col[0])
            b_stage(0, 0, *b_col[0], back[:2])
    ffn(*b_col[1])
    b_stage(1, 0, *b_col[1], back[:2])
    for p in (0, 1):
        for d in [0] + order:
            gather_wait(p, far[0], far[1], z_away(d))
    ffn(*far)
    for d in back[:2]:
        for p in (0, 1):
            b_stage(p, 1, *far, [d])

    def arrived(buffer, recv):
        pltpu.make_async_remote_copy(
            src_ref=buffer, dst_ref=buffer, send_sem=b_send.at[0, 0, 0], recv_sem=recv,
            device_id=x_next, device_id_type=pl.DeviceIdType.MESH,
        ).wait_recv()

    def reduce_a(d):
        zz = z_away(d)
        for p in (0, 1):
            yy, xx = a_col[p]
            arrived(from_b.at[p, 1, zz], b_recv.at[p, 1, zz])
            total = terms[yy, xx, zz, p].astype(F32) + from_b[p, 1, zz].astype(F32)
            terms[yy, xx, zz, p] = total.astype(BF16)
            sent.append(
                push(
                    terms.at[yy, xx, zz, p], from_a.at[p, zz],
                    a_send.at[p, zz], a_recv.at[p, zz], a_next[p],
                )
            )

    def reduce_z(d):
        zz = z_away(d)
        for p in (0, 1):
            arrived(from_b.at[p, 0, zz], b_recv.at[p, 0, zz])
            arrived(from_a.at[p, zz], a_recv.at[p, zz])
            total = (
                terms[y, x, zz, p].astype(F32)
                + from_b[p, 0, zz].astype(F32)
                + from_a[p, zz].astype(F32)
            )
            if d:
                terms[y, x, zz, p] = total.astype(BF16)
                sent.append(
                    push(
                        terms.at[y, x, zz, p], from_z.at[p, d],
                        z_send.at[p, d], z_recv.at[p, d], at(zz, y, x),
                    )
                )
            else:
                wide_hidden[p * part_rows : (p + 1) * part_rows] = (
                    wide_hidden[p * part_rows : (p + 1) * part_rows] + total
                )

    for i, d in enumerate(back):
        reduce_a(d)
        for p in (0, 1):
            if i:
                b_stage(p, 0, *b_col[p], back[i + 1 : i + 2])
            b_stage(p, 1, *far, back[i + 2 : i + 3])
        if i:
            reduce_z(back[i - 1])
    reduce_z(back[-1])
    for p in (0, 1):
        total = wide_hidden[p * part_rows : (p + 1) * part_rows]
        for d in order:
            arrived(from_z.at[p, d], z_recv.at[p, d])
            total = total + from_z[p, d].astype(F32)
        out_ref[p * part_rows : (p + 1) * part_rows] = total.astype(BF16)
    for copy in swaps + sent:
        copy.wait_send()


def per_device(
    resid_in, query_input, key_input, value_input, gate_input, decay_log, write_rate, segments,
    head_gain, out_proj, post_gain, block_exps, route_ids, route_weights, w_gate_up, w_down,
):
    tokens, width = resid_in.shape
    depth = lax.axis_size("ep") // 4
    part = tokens // 2
    hidden_units = w_down.shape[1]
    vmem = pl.BlockSpec(memory_space=pltpu.VMEM)
    hbm = pl.BlockSpec(memory_space=pl.ANY)
    dma = pltpu.SemaphoreType.DMA
    return pl.pallas_call(
        functools.partial(kernel, depth),
        out_shape=jax.ShapeDtypeStruct((tokens, width), BF16),
        in_specs=[vmem] * 13 + [hbm] * 3,
        out_specs=vmem,
        scratch_shapes=[
            pltpu.VMEM((tokens, width), BF16),
            pltpu.VMEM((2,) + out_proj.shape, BF16),
            pltpu.VMEM((2,) + w_gate_up.shape[1:], BF16),
            pltpu.VMEM((2,) + w_down.shape[1:], BF16),
            pltpu.VMEM((tokens, width), BF16),
            pltpu.VMEM((tokens, width), F32),
            pltpu.VMEM((2, 2, depth, 2, part, width + LANES), BF16),
            pltpu.VMEM((2, 2, depth, 2, part, width), BF16),
            pltpu.VMEM((2, depth * tokens, hidden_units), BF16),
            pltpu.VMEM((2, 2, depth, part, width), BF16),
            pltpu.VMEM((2, depth, part, width), BF16),
            pltpu.VMEM((2, depth, part, width), BF16),
            dma((3,)), dma((3,)), dma((3,)),
            dma((2, 4 * depth - 1)), dma((2, 4, depth)),
            dma((2, 2, depth)), dma((2, 2, depth)),
            dma((2, depth)), dma((2, depth)),
            dma((2, depth)), dma((2, depth)),
        ],
        compiler_params=pltpu.CompilerParams(
            collective_id=0, has_side_effects=True, vmem_limit_bytes=60 * 1024 * 1024
        ),
        cost_estimate=pl.CostEstimate(
            flops=14_000_000_000, bytes_accessed=24_000_000, transcendentals=2_000_000
        ),
    )(
        resid_in, query_input, key_input, value_input, gate_input, decay_log, write_rate, segments,
        head_gain.reshape(1, -1), post_gain.reshape(1, -1), block_exps.T, route_ids.T, route_weights.T,
        out_proj, w_gate_up[0], w_down[0],
    )


def solution(mesh):
    rows = P(("grp", "ep", "sub"), None)
    return jax.shard_map(
        per_device,
        mesh=mesh,
        in_specs=(
            rows, rows, rows, rows, rows,
            P(None, ("grp", "ep", "sub")),
            P(None, ("grp", "ep", "sub")),
            rows,
            P(),
            P("sub", None),
            P(),
            rows, rows, rows,
            P(("ep", "sub"), None, None),
            P(("ep", "sub"), None, None),
        ),
        out_specs=rows,
        check_vma=False,
    )
```
